32 devices in a mesh: seg: 4 (over y, core), tile: 8 (over z, x).
Axes of the slice: x: 2, y: 2, z: 4, core: 2. Of those that a mesh axis runs over, the one named last changes fastest.
Arguments:
- raw: bfloat16 [8192, 12288], P('tile', 'seg'), may hold values from -6 to 6
- filters: bfloat16 [32, 128], replicated, may hold values from -0.5 to 0.5
- weights: bfloat16 [8, 32, 4096, 128], P('tile', 'seg'), may hold values from -0.09375 to 0.09375
- blocks: int32 [8, 32], replicated, may hold values from 0 to 95, as said below
- shifts: int32 [8, 32], replicated, may hold values from 0 to 64
Outputs:
- image: bfloat16 [8, 16, 64, 4096], P('tile', None, None, 'seg')
The draws below stay inside these ranges and needn't reach their ends.
Inputs may be any that keep to these rules, and one draw needn't show every extreme that they name: Block numbers of the record's 128-channel blocks. Take any s and t, and the entries s * 8 to (s + 1) * 8 - 1 of the tiles t * 1 to (t + 1) - 1: at most 3 of them name blocks of one fibre segment (blocks k * 24 to (k + 1) * 24 - 1), and some segment is named by exactly 3 of them. A block may stand more than once in a tile's list.
All inputs are finite; a program needn't handle non-finite values.
Results may differ from the reference program's by a relative error of at most 0.0049.
Values may be sent and summed in bfloat16 or wider, within the bound.
A program may use at most 128 MiB of HBM per device.

```python
import jax
import jax.numpy as jnp
from jax import lax

C = 12288
BLOCK = 128
F = 16
TAPS = 128
FRAME_HOP = 64
S = 8192
MAXSHIFT = 64
EPD = 8
CAP = 3
TILE_DEV = 1
P_SIZE = 4096
NB = 96
L = 128
TOUT = 64
E = 32
TILES = 8


def route_tables(key):
    tile_count = TILES // TILE_DEV
    seg_count = E // EPD
    slot_count = TILE_DEV * EPD
    per_segment = C // BLOCK // seg_count
    base_key = jax.random.fold_in(key, 11)
    key_list = jax.random.split(base_key, 6)
    grid = (tile_count, seg_count)
    hot_seg = jnp.minimum(jax.random.randint(key_list[0], grid, 0, seg_count), jax.random.randint(key_list[1], grid, 0, seg_count))
    token_count = seg_count * CAP
    tokens = jnp.arange(token_count, dtype=jnp.int32) // CAP
    scores = jax.random.randint(key_list[2], grid + (token_count,), 0, 1048576) * token_count + jnp.arange(token_count, dtype=jnp.int32)
    scores = scores + jnp.where(tokens == hot_seg[..., None], 268435456, 0)
    ordering = jnp.argsort(scores, axis=-1)
    remaining = jnp.take(tokens, ordering)[..., :slot_count - CAP]
    segments = jnp.concatenate([jnp.broadcast_to(hot_seg[..., None], grid + (CAP,)), remaining], -1)
    mixing = jax.random.randint(key_list[3], grid + (slot_count,), 0, 1048576) * slot_count + jnp.arange(slot_count, dtype=jnp.int32)
    shuffle = jnp.argsort(mixing, axis=-1)
    segments = jnp.take_along_axis(segments, shuffle, -1)
    within = jax.random.randint(key_list[4], grid + (slot_count,), 0, per_segment)
    block_ids = (segments * per_segment + within).astype(jnp.int32)
    delays = jax.random.randint(key_list[5], grid + (slot_count,), 0, MAXSHIFT + 1)
    position = jnp.arange(slot_count, dtype=jnp.int32)
    delays = jnp.where(position == 0, MAXSHIFT, jnp.where(position == 1, 0, delays))
    delays = jnp.take_along_axis(delays, shuffle, -1).astype(jnp.int32)

    def arrange(table):
        return table.reshape(tile_count, seg_count, TILE_DEV, EPD).transpose(0, 2, 1, 3).reshape(TILES, E)
    return (arrange(block_ids), arrange(delays))


def draw_blocks(key, part):
    return route_tables(key)[0]


def draw_shifts(key, part):
    return route_tables(key)[1]


def block_levels(rng, shape, cuts, least, top_value):
    loudness = 1.0
    for dim, shards_of in cuts:
        steps = jax.random.uniform(jax.random.fold_in(jax.random.fold_in(rng, 6), dim), (shards_of,), jnp.float32, least / len(cuts), top_value / len(cuts))
        loudness = loudness * jnp.repeat(jnp.exp(steps), shape[dim] // shards_of).reshape((-1,) + (1,) * (len(shape) - 1 - dim))
    return loudness


def noise(stream_key, shape, spread, limit, shards=(), kind=jnp.bfloat16):
    values = spread * jax.random.normal(stream_key, shape, jnp.float32)
    if shards:
        values = values * block_levels(stream_key, shape, shards, -0.22, 0.18)
    return jnp.clip(values, -limit, limit).astype(kind)


def setup_inputs(seed: int = 0) -> dict:
    keys = jax.random.split(jax.random.key(seed), 6)
    return {
        "raw": noise(keys[0], (S, C), 1.0, 6.0, ((0, 8), (1, 4))),
        "filters": noise(keys[1], (2 * F, TAPS), TAPS ** -0.5, 0.5),
        "weights": noise(keys[2], (TILES, E, P_SIZE, BLOCK), (E * BLOCK) ** -0.5, 0.09375, ((0, 8), (1, 4))),
        "blocks": draw_blocks(jax.random.fold_in(keys[5], 71), 0),
        "shifts": draw_shifts(jax.random.fold_in(keys[5], 71), 0),
    }


def reference(raw, filters, weights, blocks, shifts):
    extended = jnp.concatenate([raw, jnp.zeros((FRAME_HOP, C), raw.dtype)], 0)
    hop_frame_rows = extended.reshape(L + 1, FRAME_HOP, C).astype(jnp.float32)
    filter_taps_full = filters.astype(jnp.float32)
    filter_bank_output = jnp.einsum('xt,stm->xsm', filter_taps_full[:, :FRAME_HOP], hop_frame_rows[:-1])
    filter_bank_output = filter_bank_output + jnp.einsum('xt,stm->xsm', filter_taps_full[:, FRAME_HOP:], hop_frame_rows[1:])
    signal_envelope = jnp.sqrt(filter_bank_output[:F] ** 2 + filter_bank_output[F:] ** 2).astype(jnp.bfloat16)
    by_block = signal_envelope.reshape(F, L, NB, BLOCK).transpose(2, 0, 1, 3)

    def one_tile(operands):
        tile_weights, tile_blocks, source_tile_delays = operands
        selected = jnp.take(by_block, tile_blocks, axis=0)
        windows = jax.vmap(lambda series, delay: lax.dynamic_slice_in_dim(series, delay, TOUT, 1))(selected, source_tile_delays)
        summed = jnp.einsum('epc,eftc->ftp', tile_weights.astype(jnp.float32), windows.astype(jnp.float32))
        return summed.astype(jnp.bfloat16)
    return lax.map(one_tile, (weights, blocks, shifts))
```

```python
import functools

import jax
import jax.numpy as jnp
from jax import lax
from jax.experimental import pallas as pl
from jax.experimental.pallas import tpu as pltpu
from jax.sharding import PartitionSpec as P

MAXSHIFT = 64
CHUNKS = 4
CORES = 2


def kernel(
    dims,
    raw_ref,
    taps_ref,
    weights_ref,
    blocks_ref,
    shifts_ref,
    out_ref,
    raw_x,
    w_all,
    onehot,
    lhs,
    picked,
    landed,
    near_s,
    near_r,
    far_s,
    far_r,
    own_s,
    own_r,
    own_f,
    mine_f,
    *rest,
):
    seg_count, tile_count, hop, frames, per_seg, entries, steps, fc = dims
    gathered = rest[:CHUNKS]
    (raw_sem, w_sem, halo_sem, g_send, g_recv, a_send, a_recv, a_loc, r_send, r_recv) = rest[CHUNKS:]
    rows = fc * frames
    out_rows = fc * steps
    samples = raw_ref.shape[0]
    part = out_ref.shape[1]
    rings = seg_count // CORES
    s = lax.axis_index("seg")
    t = lax.axis_index("tile")
    core = lax.rem(s, CORES)
    y = s // CORES
    mate = s + 1 - 2 * core

    def peer_y(dy):
        return lax.rem(y + dy, rings) * CORES + core

    def peer_t(dt):
        return lax.rem(t + dt, tile_count)

    raw_copy = pltpu.make_async_copy(raw_ref, raw_x.at[pl.ds(0, samples)], raw_sem.at[0])
    raw_copy.start()

    barrier = pltpu.get_barrier_semaphore()
    pl.semaphore_signal(barrier, inc=1, device_id={"seg": mate}, device_id_type=pl.DeviceIdType.MESH)
    for dy in range(1, rings):
        pl.semaphore_signal(
            barrier, inc=1, device_id={"seg": peer_y(dy)}, device_id_type=pl.DeviceIdType.MESH
        )
    for dt in range(1, tile_count):
        pl.semaphore_signal(
            barrier, inc=1, device_id={"tile": peer_t(dt)}, device_id_type=pl.DeviceIdType.MESH
        )
    pl.semaphore_wait(barrier, 1 + rings - 1 + tile_count - 1)

    def remote(src, dst, send, recv, **device):
        return pltpu.make_async_remote_copy(
            src_ref=src,
            dst_ref=dst,
            send_sem=send,
            recv_sem=recv,
            device_id=device,
            device_id_type=pl.DeviceIdType.MESH,
        )

    rim = pl.ds(samples, hop)
    halo = remote(
        raw_ref.at[pl.ds(0, hop)],
        raw_x.at[rim],
        halo_sem.at[0],
        halo_sem.at[1],
        tile=lax.rem(t + tile_count - 1, tile_count),
    )

    @pl.when(t > 0)
    def _():
        halo.start()

    w_copies = []
    for e in range(entries):
        copy = pltpu.make_async_copy(
            weights_ref.at[0, e], w_all.at[:, pl.ds(e * 128, 128)], w_sem.at[e]
        )
        copy.start()
        w_copies.append(copy)

    raw_copy.wait()

    @pl.when(t < tile_count - 1)
    def _():
        halo.wait_recv()

    @pl.when(t == tile_count - 1)
    def _():
        raw_x[rim, :] = jnp.zeros((hop, raw_x.shape[1]), raw_x.dtype)

    pending = []
    wide = 2 if per_seg % 2 == 0 else 1

    def own_slots(seg):
        return pl.ds(seg * per_seg, per_seg)

    def envelope(k):
        grid = gathered[k]

        def body(i, carry):
            cols = pl.ds(pl.multiple_of(i * (wide * 128), wide * 128), wide * 128)
            both = jnp.dot(taps_ref[k], raw_x[:, cols], preferred_element_type=jnp.float32)
            inphase, quadrature = both[:rows], both[rows:]
            env = jnp.sqrt(inphase * inphase + quadrature * quadrature).astype(jnp.bfloat16)
            for b in range(wide):
                grid[s * per_seg + i * wide + b] = env[:, b * 128 : (b + 1) * 128]
            return carry

        lax.fori_loop(0, per_seg // wide, body, 0)
        held = grid.at[own_slots(s)]
        copies = []
        for dy in range(1, rings):
            copies.append(remote(held, held, g_send.at[k, dy], g_recv.at[k, dy], seg=peer_y(dy)))
        copies.append(remote(held, held, g_send.at[k, 0], g_recv.at[k, 0], seg=mate))
        for copy in copies:
            copy.start()
        pending.extend(copies)
        return copies

    def exchange(k, copies):
        grid = gathered[k]
        forwards = []
        for dy in range(1, rings):
            copies[dy - 1].wait_recv()
            origin = lax.rem(y + rings - dy, rings) * CORES + core
            held = grid.at[own_slots(origin)]
            copy = remote(
                held, held, g_send.at[k, rings + dy - 1], g_recv.at[k, rings + dy - 1], seg=mate
            )
            copy.start()
            forwards.append(copy)
        copies[-1].wait_recv()
        for copy in forwards:
            copy.wait_recv()
        pending.extend(forwards)

        def pick(j, carry):
            for e in range(entries):
                picked[k, j, e] = grid[blocks_ref[j, s * entries + e]]
            return carry

        lax.fori_loop(0, tile_count, pick, 0)
        sent = []
        order = sorted(range(1, tile_count), key=lambda dt: -min(dt, tile_count - dt))
        for dt in order:
            copy = remote(
                picked.at[k, peer_t(dt)],
                landed.at[k, t],
                a_send.at[k, dt],
                a_recv.at[k, dt],
                tile=peer_t(dt),
            )
            copy.start()
            sent.append(copy)
        local = pltpu.make_async_copy(picked.at[k, t], landed.at[k, t], a_loc.at[k])
        local.start()
        pending.extend(sent)
        return sent, local

    def make_onehot():
        shape = (out_rows, tile_count * rows)
        m = lax.broadcasted_iota(jnp.int32, shape, 0)
        n = lax.broadcasted_iota(jnp.int32, shape, 1)
        frame = (n // rows) * frames + n % frames
        gap = jnp.where(m // steps == (n // frames) % fc, frame - m % steps, -1)

        def body(e, carry):
            d = shifts_ref[t, s * entries + e]
            onehot[e] = jnp.where(gap == d, 1.0, 0.0).astype(jnp.bfloat16)
            return carry

        lax.fori_loop(0, entries, body, 0)

    tile_p = min(256, part)

    def multiply(q, store):
        def body(i, carry):
            start = pl.multiple_of(i * tile_p, tile_p)
            value = lax.dot_general(
                lhs[...],
                w_all[pl.ds(pl.multiple_of(q * part + start, tile_p), tile_p), :],
                (((1,), (1,)), ((), ())),
                preferred_element_type=jnp.float32,
            )
            store(pl.ds(start, tile_p), value)
            return carry

        lax.fori_loop(0, part // tile_p, body, 0)

    def stack(k, arrivals):
        sent, local = arrivals
        for copy in sent:
            copy.wait_recv()
        local.wait()

        def shift(e, carry):
            series = landed[k, :, e].reshape(tile_count * rows, 128)
            lanes = pl.ds(pl.multiple_of(e * 128, 128), 128)
            lhs[:, lanes] = jnp.dot(
                onehot[e], series, preferred_element_type=jnp.float32
            ).astype(jnp.bfloat16)
            return carry

        lax.fori_loop(0, entries, shift, 0)
        if k == 0:
            for copy in w_copies:
                copy.wait()
        far = []
        for dy in range(1, rings):
            yy = lax.rem(y + dy, rings)
            i = dy - 1

            def put_near(cols, value):
                near_s[k, i, :, cols] = value.astype(jnp.bfloat16)

            multiply(yy * CORES + 1 - core, put_near)
            near = remote(near_s.at[k, i], near_r.at[k, i], r_send.at[k, i], r_recv.at[k, i], seg=mate)
            near.start()

            def put_mine(cols, value):
                mine_f[:, cols] = value

            multiply(yy * CORES + core, put_mine)
            near.wait_recv()
            far_s[k, i] = (mine_f[...] + near_r[k, i].astype(jnp.float32)).astype(jnp.bfloat16)
            copy = remote(
                far_s.at[k, i],
                far_r.at[k, i],
                r_send.at[k, rings - 1 + i],
                r_recv.at[k, rings - 1 + i],
                seg=peer_y(dy),
            )
            copy.start()
            far.append(copy)
            pending.append(near)

        def put_own(cols, value):
            own_s[k, :, cols] = value.astype(jnp.bfloat16)

        multiply(y * CORES + 1 - core, put_own)
        own = remote(
            own_s.at[k], own_r.at[k], r_send.at[k, 2 * rings - 2], r_recv.at[k, 2 * rings - 2], seg=mate
        )
        own.start()

        def keep(cols, value):
            own_f[k, :, cols] = value

        multiply(s, keep)
        pending.extend(far)
        pending.append(own)
        return far, own

    def finish(k, sums):
        far, own = sums
        own.wait_recv()
        total = own_f[k] + own_r[k].astype(jnp.float32)
        for i, copy in enumerate(far):
            copy.wait_recv()
            total = total + far_r[k, i].astype(jnp.float32)
        out_ref[pl.ds(k * out_rows, out_rows), :] = total.astype(jnp.bfloat16)

    gathers = {}
    arrivals = {}
    gathers[0] = envelope(0)
    for k in range(CHUNKS):
        if k + 1 < CHUNKS:
            gathers[k + 1] = envelope(k + 1)
        arrivals[k] = exchange(k, gathers[k])
    make_onehot()
    sums = {}
    for k in range(CHUNKS):
        sums[k] = stack(k, arrivals[k])
        if k:
            finish(k - 1, sums[k - 1])
    finish(CHUNKS - 1, sums[CHUNKS - 1])

    for copy in pending:
        copy.wait_send()

    @pl.when(t > 0)
    def _():
        halo.wait_send()


def local(raw, filters, weights, blocks, shifts):
    seg_count = lax.axis_size("seg")
    tile_count = lax.axis_size("tile")
    samples, channels = raw.shape
    taps = filters.shape[1]
    hop = taps // 2
    bank = filters.shape[0] // 2
    per_seg = channels // weights.shape[3]
    frames = samples // hop
    entries = weights.shape[1]
    points = weights.shape[2]
    part = points // seg_count
    steps = tile_count * frames - MAXSHIFT
    fc = bank // CHUNKS
    rows = fc * frames
    out_rows = fc * steps
    rings = seg_count // CORES
    depth = samples + hop
    bf16 = jnp.bfloat16
    banded = jnp.stack(
        [
            jnp.pad(filters, ((0, 0), (hop * i, depth - taps - hop * i)))
            for i in range(frames)
        ],
        1,
    )
    banded = (
        banded.reshape(2, CHUNKS, fc, frames, depth)
        .transpose(1, 0, 2, 3, 4)
        .reshape(CHUNKS, 2 * rows, depth)
    )
    dims = (seg_count, tile_count, hop, frames, per_seg, entries, steps, fc)
    other = max(rings - 1, 1)
    image = pl.pallas_call(
        functools.partial(kernel, dims),
        out_shape=jax.ShapeDtypeStruct((CHUNKS * out_rows, part), bf16),
        in_specs=[
            pl.BlockSpec(memory_space=pl.ANY),
            pl.BlockSpec(memory_space=pltpu.VMEM),
            pl.BlockSpec(memory_space=pl.ANY),
            pl.BlockSpec(memory_space=pltpu.SMEM),
            pl.BlockSpec(memory_space=pltpu.SMEM),
        ],
        out_specs=pl.BlockSpec(memory_space=pltpu.VMEM),
        scratch_shapes=[
            pltpu.VMEM((depth, channels), bf16),
            pltpu.VMEM((points, entries * 128), bf16),
            pltpu.VMEM((entries, out_rows, tile_count * rows), bf16),
            pltpu.VMEM((out_rows, entries * 128), bf16),
            pltpu.VMEM((CHUNKS, tile_count, entries, rows, 128), bf16),
            pltpu.VMEM((CHUNKS, tile_count, entries, rows, 128), bf16),
            pltpu.VMEM((CHUNKS, other, out_rows, part), bf16),
            pltpu.VMEM((CHUNKS, other, out_rows, part), bf16),
            pltpu.VMEM((CHUNKS, other, out_rows, part), bf16),
            pltpu.VMEM((CHUNKS, other, out_rows, part), bf16),
            pltpu.VMEM((CHUNKS, out_rows, part), bf16),
            pltpu.VMEM((CHUNKS, out_rows, part), bf16),
            pltpu.VMEM((CHUNKS, out_rows, part), jnp.float32),
            pltpu.VMEM((out_rows, part), jnp.float32),
            *[pltpu.VMEM((seg_count * per_seg, rows, 128), bf16) for _ in range(CHUNKS)],
            pltpu.SemaphoreType.DMA((1,)),
            pltpu.SemaphoreType.DMA((entries,)),
            pltpu.SemaphoreType.DMA((2,)),
            pltpu.SemaphoreType.DMA((CHUNKS, 2 * rings)),
            pltpu.SemaphoreType.DMA((CHUNKS, 2 * rings)),
            pltpu.SemaphoreType.DMA((CHUNKS, tile_count)),
            pltpu.SemaphoreType.DMA((CHUNKS, tile_count)),
            pltpu.SemaphoreType.DMA((CHUNKS,)),
            pltpu.SemaphoreType.DMA((CHUNKS, 2 * rings)),
            pltpu.SemaphoreType.DMA((CHUNKS, 2 * rings)),
        ],
        compiler_params=pltpu.CompilerParams(
            collective_id=0, has_side_effects=True, vmem_limit_bytes=60 * 1024 * 1024
        ),
    )(raw, banded, weights, blocks, shifts)
    return image.reshape(1, bank, steps, part)


def solution(mesh):
    return jax.shard_map(
        local,
        mesh=mesh,
        in_specs=(P("tile", "seg"), P(), P("tile", "seg", None, None), P(), P()),
        out_specs=P("tile", None, None, "seg"),
        check_vma=False,
    )
```

```python
import functools

import jax
import jax.numpy as jnp
from jax import lax
from jax.experimental import pallas as pl
from jax.experimental.pallas import tpu as pltpu
from jax.sharding import PartitionSpec as P

MAXSHIFT = 64
CHUNKS = 8
CORES = 2


def kernel(
    dims,
    raw_ref,
    taps_ref,
    weights_ref,
    blocks_ref,
    shifts_ref,
    out_ref,
    raw_x,
    w_all,
    onehot,
    lhs,
    picked,
    landed,
    near_s,
    near_r,
    far_s,
    far_r,
    own_s,
    own_r,
    own_f,
    mine_f,
    band,
    *rest,
):
    seg_count, tile_count, hop, frames, per_seg, entries, steps, fc = dims
    gathered = rest[:CHUNKS]
    (raw_sem, w_sem, halo_sem, g_send, g_recv, a_send, a_recv, a_loc, r_send, r_recv) = rest[CHUNKS:]
    rows = fc * frames
    out_rows = fc * steps
    samples = raw_ref.shape[0]
    part = out_ref.shape[1]
    rings = seg_count // CORES
    s = lax.axis_index("seg")
    t = lax.axis_index("tile")
    core = lax.rem(s, CORES)
    y = s // CORES
    mate = s + 1 - 2 * core

    def peer_y(dy):
        return lax.rem(y + dy, rings) * CORES + core

    def peer_t(dt):
        return lax.rem(t + dt, tile_count)

    raw_copy = pltpu.make_async_copy(raw_ref, raw_x.at[pl.ds(0, samples)], raw_sem.at[0])
    raw_copy.start()

    barrier = pltpu.get_barrier_semaphore()
    pl.semaphore_signal(barrier, inc=1, device_id={"seg": mate}, device_id_type=pl.DeviceIdType.MESH)
    for dy in range(1, rings):
        pl.semaphore_signal(
            barrier, inc=1, device_id={"seg": peer_y(dy)}, device_id_type=pl.DeviceIdType.MESH
        )
    for dt in range(1, tile_count):
        pl.semaphore_signal(
            barrier, inc=1, device_id={"tile": peer_t(dt)}, device_id_type=pl.DeviceIdType.MESH
        )
    pl.semaphore_wait(barrier, 1 + rings - 1 + tile_count - 1)

    def remote(src, dst, send, recv, **device):
        return pltpu.make_async_remote_copy(
            src_ref=src,
            dst_ref=dst,
            send_sem=send,
            recv_sem=recv,
            device_id=device,
            device_id_type=pl.DeviceIdType.MESH,
        )

    rim = pl.ds(samples, hop)
    halo = remote(
        raw_ref.at[pl.ds(0, hop)],
        raw_x.at[rim],
        halo_sem.at[0],
        halo_sem.at[1],
        tile=lax.rem(t + tile_count - 1, tile_count),
    )

    @pl.when(t > 0)
    def _():
        halo.start()

    w_copies = []
    for e in range(entries):
        copy = pltpu.make_async_copy(
            weights_ref.at[0, e], w_all.at[:, pl.ds(e * 128, 128)], w_sem.at[e]
        )
        copy.start()
        w_copies.append(copy)

    pending = []
    wide = 2 if per_seg % 2 == 0 else 1

    def own_slots(seg):
        return pl.ds(seg * per_seg, per_seg)

    def make_band(k):
        bank = taps_ref.shape[0]
        row = lax.broadcasted_iota(jnp.int32, (2 * rows, bank), 0)
        col = lax.broadcasted_iota(jnp.int32, (2 * rows, bank), 1)
        wanted = (row // rows) * (bank // 2) + k * fc + (row // frames) % fc
        pick_rows = jnp.where(wanted == col, 1.0, 0.0).astype(jnp.bfloat16)
        taps = jnp.dot(pick_rows, taps_ref[...], preferred_element_type=jnp.float32)
        turned = jnp.concatenate([taps[:, hop:], taps[:, :hop]], 1)
        frame = lax.broadcasted_iota(jnp.int32, taps.shape, 0) % frames
        lane = lax.broadcasted_iota(jnp.int32, taps.shape, 1)
        for m in range((samples + hop + 2 * hop - 1) // (2 * hop)):
            left = m * 2 * hop
            width = min(2 * hop, samples + hop - left)
            odd = frame == jnp.where(lane < hop, 2 * m - 1, 2 * m + 1)
            value = jnp.where(frame == 2 * m, taps, jnp.where(odd, turned, 0.0))
            band[:, left : left + width] = value[:, :width].astype(jnp.bfloat16)

    def envelope(k):
        grid = gathered[k]

        def body(i, carry):
            cols = pl.ds(pl.multiple_of(i * (wide * 128), wide * 128), wide * 128)
            both = jnp.dot(band[...], raw_x[:, cols], preferred_element_type=jnp.float32)
            inphase, quadrature = both[:rows], both[rows:]
            env = jnp.sqrt(inphase * inphase + quadrature * quadrature).astype(jnp.bfloat16)
            for b in range(wide):
                grid[s * per_seg + i * wide + b] = env[:, b * 128 : (b + 1) * 128]
            return carry

        if k:
            make_band(k)
        lax.fori_loop(0, per_seg // wide, body, 0)
        held = grid.at[own_slots(s)]
        copies = []
        for dy in range(1, rings):
            copies.append(remote(held, held, g_send.at[k, dy], g_recv.at[k, dy], seg=peer_y(dy)))
        copies.append(remote(held, held, g_send.at[k, 0], g_recv.at[k, 0], seg=mate))
        for copy in copies:
            copy.start()
        pending.extend(copies)
        return copies

    def exchange(k, copies):
        grid = gathered[k]
        forwards = []
        for dy in range(1, rings):
            copies[dy - 1].wait_recv()
            origin = lax.rem(y + rings - dy, rings) * CORES + core
            held = grid.at[own_slots(origin)]
            copy = remote(
                held, held, g_send.at[k, rings + dy - 1], g_recv.at[k, rings + dy - 1], seg=mate
            )
            copy.start()
            forwards.append(copy)
        copies[-1].wait_recv()
        for copy in forwards:
            copy.wait_recv()
        pending.extend(forwards)

        def pick(j, carry):
            for e in range(entries):
                picked[k, j, e] = grid[blocks_ref[j, s * entries + e]]
            return carry

        lax.fori_loop(0, tile_count, pick, 0)
        sent = []
        order = sorted(range(1, tile_count), key=lambda dt: -min(dt, tile_count - dt))
        for dt in order:
            copy = remote(
                picked.at[k, peer_t(dt)],
                landed.at[k, t],
                a_send.at[k, dt],
                a_recv.at[k, dt],
                tile=peer_t(dt),
            )
            copy.start()
            sent.append(copy)
        local = pltpu.make_async_copy(picked.at[k, t], landed.at[k, t], a_loc.at[k])
        local.start()
        pending.extend(sent)
        return sent, local

    def make_onehot():
        shape = (out_rows, tile_count * rows)
        m = lax.broadcasted_iota(jnp.int32, shape, 0)
        n = lax.broadcasted_iota(jnp.int32, shape, 1)
        frame = (n // rows) * frames + n % frames
        gap = jnp.where(m // steps == (n // frames) % fc, frame - m % steps, -1)

        def body(e, carry):
            d = shifts_ref[t, s * entries + e]
            onehot[e] = jnp.where(gap == d, 1.0, 0.0).astype(jnp.bfloat16)
            return carry

        lax.fori_loop(0, entries, body, 0)

    tile_p = min(256, part)

    def multiply(q, store):
        def body(i, carry):
            start = pl.multiple_of(i * tile_p, tile_p)
            value = lax.dot_general(
                lhs[...],
                w_all[pl.ds(pl.multiple_of(q * part + start, tile_p), tile_p), :],
                (((1,), (1,)), ((), ())),
                preferred_element_type=jnp.float32,
            )
            store(pl.ds(start, tile_p), value)
            return carry

        lax.fori_loop(0, part // tile_p, body, 0)

    def stack(k, arrivals):
        sent, local = arrivals
        for copy in sent:
            copy.wait_recv()
        local.wait()

        def shift(e, carry):
            series = landed[k, :, e].reshape(tile_count * rows, 128)
            lanes = pl.ds(pl.multiple_of(e * 128, 128), 128)
            lhs[:, lanes] = jnp.dot(
                onehot[e], series, preferred_element_type=jnp.float32
            ).astype(jnp.bfloat16)
            return carry

        lax.fori_loop(0, entries, shift, 0)
        if k == 0:
            for copy in w_copies:
                copy.wait()
        far = []
        for dy in range(1, rings):
            yy = lax.rem(y + dy, rings)
            i = dy - 1

            def put_near(cols, value):
                near_s[k, i, :, cols] = value.astype(jnp.bfloat16)

            multiply(yy * CORES + 1 - core, put_near)
            near = remote(near_s.at[k, i], near_r.at[k, i], r_send.at[k, i], r_recv.at[k, i], seg=mate)
            near.start()

            def put_mine(cols, value):
                mine_f[:, cols] = value

            multiply(yy * CORES + core, put_mine)
            near.wait_recv()
            far_s[k, i] = (mine_f[...] + near_r[k, i].astype(jnp.float32)).astype(jnp.bfloat16)
            copy = remote(
                far_s.at[k, i],
                far_r.at[k, i],
                r_send.at[k, rings - 1 + i],
                r_recv.at[k, rings - 1 + i],
                seg=peer_y(dy),
            )
            copy.start()
            far.append(copy)
            pending.append(near)

        def put_own(cols, value):
            own_s[k, :, cols] = value.astype(jnp.bfloat16)

        multiply(y * CORES + 1 - core, put_own)
        own = remote(
            own_s.at[k], own_r.at[k], r_send.at[k, 2 * rings - 2], r_recv.at[k, 2 * rings - 2], seg=mate
        )
        own.start()

        def keep(cols, value):
            own_f[k, :, cols] = value

        multiply(s, keep)
        pending.extend(far)
        pending.append(own)
        return far, own

    def finish(k, sums):
        far, own = sums
        own.wait_recv()
        total = own_f[k] + own_r[k].astype(jnp.float32)
        for i, copy in enumerate(far):
            copy.wait_recv()
            total = total + far_r[k, i].astype(jnp.float32)
        out_ref[pl.ds(k * out_rows, out_rows), :] = total.astype(jnp.bfloat16)

    make_band(0)
    make_onehot()
    raw_copy.wait()

    @pl.when(t < tile_count - 1)
    def _():
        halo.wait_recv()

    @pl.when(t == tile_count - 1)
    def _():
        raw_x[rim, :] = jnp.zeros((hop, raw_x.shape[1]), raw_x.dtype)

    gathers = {}
    arrivals = {}
    gathers[0] = envelope(0)
    for k in range(CHUNKS):
        if k + 1 < CHUNKS:
            gathers[k + 1] = envelope(k + 1)
        arrivals[k] = exchange(k, gathers[k])
    sums = {}
    for k in range(CHUNKS):
        sums[k] = stack(k, arrivals[k])
        if k:
            finish(k - 1, sums[k - 1])
    finish(CHUNKS - 1, sums[CHUNKS - 1])

    for copy in pending:
        copy.wait_send()

    @pl.when(t > 0)
    def _():
        halo.wait_send()


def local(raw, filters, weights, blocks, shifts):
    seg_count = lax.axis_size("seg")
    tile_count = lax.axis_size("tile")
    samples, channels = raw.shape
    taps = filters.shape[1]
    hop = taps // 2
    bank = filters.shape[0] // 2
    per_seg = channels // weights.shape[3]
    frames = samples // hop
    entries = weights.shape[1]
    points = weights.shape[2]
    part = points // seg_count
    steps = tile_count * frames - MAXSHIFT
    fc = bank // CHUNKS
    rows = fc * frames
    out_rows = fc * steps
    rings = seg_count // CORES
    depth = samples + hop
    bf16 = jnp.bfloat16
    dims = (seg_count, tile_count, hop, frames, per_seg, entries, steps, fc)
    other = max(rings - 1, 1)
    image = pl.pallas_call(
        functools.partial(kernel, dims),
        out_shape=jax.ShapeDtypeStruct((CHUNKS * out_rows, part), bf16),
        in_specs=[
            pl.BlockSpec(memory_space=pl.ANY),
            pl.BlockSpec(memory_space=pltpu.VMEM),
            pl.BlockSpec(memory_space=pl.ANY),
            pl.BlockSpec(memory_space=pltpu.SMEM),
            pl.BlockSpec(memory_space=pltpu.SMEM),
        ],
        out_specs=pl.BlockSpec(memory_space=pltpu.VMEM),
        scratch_shapes=[
            pltpu.VMEM((depth, channels), bf16),
            pltpu.VMEM((points, entries * 128), bf16),
            pltpu.VMEM((entries, out_rows, tile_count * rows), bf16),
            pltpu.VMEM((out_rows, entries * 128), bf16),
            pltpu.VMEM((CHUNKS, tile_count, entries, rows, 128), bf16),
            pltpu.VMEM((CHUNKS, tile_count, entries, rows, 128), bf16),
            pltpu.VMEM((CHUNKS, other, out_rows, part), bf16),
            pltpu.VMEM((CHUNKS, other, out_rows, part), bf16),
            pltpu.VMEM((CHUNKS, other, out_rows, part), bf16),
            pltpu.VMEM((CHUNKS, other, out_rows, part), bf16),
            pltpu.VMEM((CHUNKS, out_rows, part), bf16),
            pltpu.VMEM((CHUNKS, out_rows, part), bf16),
            pltpu.VMEM((CHUNKS, out_rows, part), jnp.float32),
            pltpu.VMEM((out_rows, part), jnp.float32),
            pltpu.VMEM((2 * rows, depth), bf16),
            *[pltpu.VMEM((seg_count * per_seg, rows, 128), bf16) for _ in range(CHUNKS)],
            pltpu.SemaphoreType.DMA((1,)),
            pltpu.SemaphoreType.DMA((entries,)),
            pltpu.SemaphoreType.DMA((2,)),
            pltpu.SemaphoreType.DMA((CHUNKS, 2 * rings)),
            pltpu.SemaphoreType.DMA((CHUNKS, 2 * rings)),
            pltpu.SemaphoreType.DMA((CHUNKS, tile_count)),
            pltpu.SemaphoreType.DMA((CHUNKS, tile_count)),
            pltpu.SemaphoreType.DMA((CHUNKS,)),
            pltpu.SemaphoreType.DMA((CHUNKS, 2 * rings)),
            pltpu.SemaphoreType.DMA((CHUNKS, 2 * rings)),
        ],
        compiler_params=pltpu.CompilerParams(
            collective_id=0, has_side_effects=True, vmem_limit_bytes=60 * 1024 * 1024
        ),
    )(raw, filters, weights, blocks, shifts)
    return image.reshape(1, bank, steps, part)


def solution(mesh):
    return jax.shard_map(
        local,
        mesh=mesh,
        in_specs=(P("tile", "seg"), P(), P("tile", "seg", None, None), P(), P()),
        out_specs=P("tile", None, None, "seg"),
        check_vma=False,
    )
```

```python
import functools

import jax
import jax.numpy as jnp
from jax import lax
from jax.experimental import pallas as pl
from jax.experimental.pallas import tpu as pltpu
from jax.sharding import PartitionSpec as P

MAXSHIFT = 64
CHUNKS = 8
CORES = 2


def kernel(
    dims,
    raw_ref,
    taps_ref,
    weights_ref,
    blocks_ref,
    shifts_ref,
    out_ref,
    raw_x,
    w_all,
    onehot,
    lhs,
    picked,
    landed,
    near_s,
    near_r,
    far_s,
    far_r,
    own_s,
    own_r,
    own_f,
    mine_f,
    band,
    *rest,
):
    seg_count, tile_count, hop, frames, per_seg, entries, steps, fc = dims
    gathered = rest[:CHUNKS]
    (raw_sem, w_sem, halo_sem, g_send, g_recv, a_send, a_recv, a_loc, r_send, r_recv) = rest[CHUNKS:]
    rows = fc * frames
    out_rows = fc * steps
    samples = raw_ref.shape[0]
    part = out_ref.shape[1]
    rings = seg_count // CORES
    s = lax.axis_index("seg")
    t = lax.axis_index("tile")
    core = lax.rem(s, CORES)
    y = s // CORES
    mate = s + 1 - 2 * core

    def peer_y(dy):
        return lax.rem(y + dy, rings) * CORES + core

    def peer_t(dt):
        if tile_count & (tile_count - 1):
            return lax.rem(t + dt, tile_count)
        peer, weight = 0, 1
        while weight < tile_count:
            bit = (t // weight) % 2
            peer = peer + weight * (1 - bit if dt & weight else bit)
            weight *= 2
        return peer

    raw_copy = pltpu.make_async_copy(raw_ref, raw_x.at[pl.ds(0, samples)], raw_sem.at[0])
    raw_copy.start()

    barrier = pltpu.get_barrier_semaphore()
    pl.semaphore_signal(barrier, inc=1, device_id={"seg": mate}, device_id_type=pl.DeviceIdType.MESH)
    for dy in range(1, rings):
        pl.semaphore_signal(
            barrier, inc=1, device_id={"seg": peer_y(dy)}, device_id_type=pl.DeviceIdType.MESH
        )
    for dt in range(1, tile_count):
        pl.semaphore_signal(
            barrier, inc=1, device_id={"tile": peer_t(dt)}, device_id_type=pl.DeviceIdType.MESH
        )
    pl.semaphore_wait(barrier, 1 + rings - 1 + tile_count - 1)

    def remote(src, dst, send, recv, **device):
        return pltpu.make_async_remote_copy(
            src_ref=src,
            dst_ref=dst,
            send_sem=send,
            recv_sem=recv,
            device_id=device,
            device_id_type=pl.DeviceIdType.MESH,
        )

    rim = pl.ds(samples, hop)
    halo = remote(
        raw_ref.at[pl.ds(0, hop)],
        raw_x.at[rim],
        halo_sem.at[0],
        halo_sem.at[1],
        tile=lax.rem(t + tile_count - 1, tile_count),
    )

    @pl.when(t > 0)
    def _():
        halo.start()

    w_copies = []
    for e in range(entries):
        copy = pltpu.make_async_copy(
            weights_ref.at[0, e], w_all.at[:, pl.ds(e * 128, 128)], w_sem.at[e]
        )
        copy.start()
        w_copies.append(copy)

    pending = []
    wide = next(w for w in (6, 4, 3, 2, 1) if per_seg % w == 0)

    def own_slots(seg):
        return pl.ds(seg * per_seg, per_seg)

    def make_band(k):
        bank = taps_ref.shape[0]
        row = lax.broadcasted_iota(jnp.int32, (2 * rows, bank), 0)
        col = lax.broadcasted_iota(jnp.int32, (2 * rows, bank), 1)
        wanted = (row // rows) * (bank // 2) + k * fc + (row // frames) % fc
        pick_rows = jnp.where(wanted == col, 1.0, 0.0).astype(jnp.bfloat16)
        taps = jnp.dot(pick_rows, taps_ref[...], preferred_element_type=jnp.float32)
        turned = jnp.concatenate([taps[:, hop:], taps[:, :hop]], 1)
        frame = lax.broadcasted_iota(jnp.int32, taps.shape, 0) % frames
        lane = lax.broadcasted_iota(jnp.int32, taps.shape, 1)
        for m in range((samples + hop + 2 * hop - 1) // (2 * hop)):
            left = m * 2 * hop
            width = min(2 * hop, samples + hop - left)
            odd = frame == jnp.where(lane < hop, 2 * m - 1, 2 * m + 1)
            value = jnp.where(frame == 2 * m, taps, jnp.where(odd, turned, 0.0))
            band[:, left : left + width] = value[:, :width].astype(jnp.bfloat16)

    def envelope(k):
        grid = gathered[k]

        def body(i, carry):
            cols = pl.ds(pl.multiple_of(i * (wide * 128), wide * 128), wide * 128)
            both = jnp.dot(band[...], raw_x[:, cols], preferred_element_type=jnp.float32)
            inphase, quadrature = both[:rows], both[rows:]
            env = jnp.sqrt(inphase * inphase + quadrature * quadrature).astype(jnp.bfloat16)
            for b in range(wide):
                grid[s * per_seg + i * wide + b] = env[:, b * 128 : (b + 1) * 128]
            return carry

        if k:
            make_band(k)
        lax.fori_loop(0, per_seg // wide, body, 0)
        held = grid.at[own_slots(s)]
        copies = []
        for dy in range(1, rings):
            copies.append(remote(held, held, g_send.at[k, dy], g_recv.at[k, dy], seg=peer_y(dy)))
        copies.append(remote(held, held, g_send.at[k, 0], g_recv.at[k, 0], seg=mate))
        for copy in copies:
            copy.start()
        pending.extend(copies)
        return copies

    def exchange(k, copies):
        grid = gathered[k]
        forwards = []
        for dy in range(1, rings):
            copies[dy - 1].wait_recv()
            origin = lax.rem(y + rings - dy, rings) * CORES + core
            held = grid.at[own_slots(origin)]
            copy = remote(
                held, held, g_send.at[k, rings + dy - 1], g_recv.at[k, rings + dy - 1], seg=mate
            )
            copy.start()
            forwards.append(copy)
        copies[-1].wait_recv()
        for copy in forwards:
            copy.wait_recv()
        pending.extend(forwards)

        def pick(j, carry):
            for e in range(entries):
                picked[k, j, e] = grid[blocks_ref[j, s * entries + e]]
            return carry

        lax.fori_loop(0, tile_count, pick, 0)
        sent = []
        order = sorted(range(1, tile_count), key=lambda dt: -dt)
        for dt in order:
            copy = remote(
                picked.at[k, peer_t(dt)],
                landed.at[k, t],
                a_send.at[k, dt],
                a_recv.at[k, dt],
                tile=peer_t(dt),
            )
            copy.start()
            sent.append(copy)
        local = pltpu.make_async_copy(picked.at[k, t], landed.at[k, t], a_loc.at[k])
        local.start()
        pending.extend(sent)
        return sent, local

    def make_onehot():
        shape = (out_rows, tile_count * rows)
        m = lax.broadcasted_iota(jnp.int32, shape, 0)
        n = lax.broadcasted_iota(jnp.int32, shape, 1)
        frame = (n // rows) * frames + n % frames
        gap = jnp.where(m // steps == (n // frames) % fc, frame - m % steps, -1)

        def body(e, carry):
            d = shifts_ref[t, s * entries + e]
            onehot[e] = jnp.where(gap == d, 1.0, 0.0).astype(jnp.bfloat16)
            return carry

        lax.fori_loop(0, entries, body, 0)

    tile_p = min(256, part)

    def multiply(q, store):
        def body(i, carry):
            start = pl.multiple_of(i * tile_p, tile_p)
            value = lax.dot_general(
                lhs[...],
                w_all[pl.ds(pl.multiple_of(q * part + start, tile_p), tile_p), :],
                (((1,), (1,)), ((), ())),
                preferred_element_type=jnp.float32,
            )
            store(pl.ds(start, tile_p), value)
            return carry

        lax.fori_loop(0, part // tile_p, body, 0)

    def stack(k, arrivals):
        sent, local = arrivals
        for copy in sent:
            copy.wait_recv()
        local.wait()

        def shift(e, carry):
            series = landed[k, :, e].reshape(tile_count * rows, 128)
            lanes = pl.ds(pl.multiple_of(e * 128, 128), 128)
            lhs[:, lanes] = jnp.dot(
                onehot[e], series, preferred_element_type=jnp.float32
            ).astype(jnp.bfloat16)
            return carry

        lax.fori_loop(0, entries, shift, 0)
        if k == 0:
            for copy in w_copies:
                copy.wait()
        far = []
        for dy in range(1, rings):
            yy = lax.rem(y + dy, rings)
            i = dy - 1

            def put_near(cols, value):
                near_s[k, i, :, cols] = value.astype(jnp.bfloat16)

            multiply(yy * CORES + 1 - core, put_near)
            near = remote(near_s.at[k, i], near_r.at[k, i], r_send.at[k, i], r_recv.at[k, i], seg=mate)
            near.start()

            def put_mine(cols, value):
                mine_f[:, cols] = value

            multiply(yy * CORES + core, put_mine)
            near.wait_recv()
            far_s[k, i] = (mine_f[...] + near_r[k, i].astype(jnp.float32)).astype(jnp.bfloat16)
            copy = remote(
                far_s.at[k, i],
                far_r.at[k, i],
                r_send.at[k, rings - 1 + i],
                r_recv.at[k, rings - 1 + i],
                seg=peer_y(dy),
            )
            copy.start()
            far.append(copy)
            pending.append(near)

        def put_own(cols, value):
            own_s[k, :, cols] = value.astype(jnp.bfloat16)

        multiply(y * CORES + 1 - core, put_own)
        own = remote(
            own_s.at[k], own_r.at[k], r_send.at[k, 2 * rings - 2], r_recv.at[k, 2 * rings - 2], seg=mate
        )
        own.start()

        def keep(cols, value):
            own_f[k, :, cols] = value

        multiply(s, keep)
        pending.extend(far)
        pending.append(own)
        return far, own

    def finish(k, sums):
        far, own = sums
        own.wait_recv()
        total = own_f[k] + own_r[k].astype(jnp.float32)
        for i, copy in enumerate(far):
            copy.wait_recv()
            total = total + far_r[k, i].astype(jnp.float32)
        out_ref[pl.ds(k * out_rows, out_rows), :] = total.astype(jnp.bfloat16)

    make_band(0)
    make_onehot()
    raw_copy.wait()

    @pl.when(t < tile_count - 1)
    def _():
        halo.wait_recv()

    @pl.when(t == tile_count - 1)
    def _():
        raw_x[rim, :] = jnp.zeros((hop, raw_x.shape[1]), raw_x.dtype)

    gathers = {}
    arrivals = {}
    gathers[0] = envelope(0)
    for k in range(CHUNKS):
        if k + 1 < CHUNKS:
            gathers[k + 1] = envelope(k + 1)
        arrivals[k] = exchange(k, gathers[k])
    sums = {}
    for k in range(CHUNKS):
        sums[k] = stack(k, arrivals[k])
        if k:
            finish(k - 1, sums[k - 1])
    finish(CHUNKS - 1, sums[CHUNKS - 1])

    for copy in pending:
        copy.wait_send()

    @pl.when(t > 0)
    def _():
        halo.wait_send()


def local(raw, filters, weights, blocks, shifts):
    seg_count = lax.axis_size("seg")
    tile_count = lax.axis_size("tile")
    samples, channels = raw.shape
    taps = filters.shape[1]
    hop = taps // 2
    bank = filters.shape[0] // 2
    per_seg = channels // weights.shape[3]
    frames = samples // hop
    entries = weights.shape[1]
    points = weights.shape[2]
    part = points // seg_count
    steps = tile_count * frames - MAXSHIFT
    fc = bank // CHUNKS
    rows = fc * frames
    out_rows = fc * steps
    rings = seg_count // CORES
    depth = samples + hop
    bf16 = jnp.bfloat16
    dims = (seg_count, tile_count, hop, frames, per_seg, entries, steps, fc)
    other = max(rings - 1, 1)
    image = pl.pallas_call(
        functools.partial(kernel, dims),
        out_shape=jax.ShapeDtypeStruct((CHUNKS * out_rows, part), bf16),
        in_specs=[
            pl.BlockSpec(memory_space=pl.ANY),
            pl.BlockSpec(memory_space=pltpu.VMEM),
            pl.BlockSpec(memory_space=pl.ANY),
            pl.BlockSpec(memory_space=pltpu.SMEM),
            pl.BlockSpec(memory_space=pltpu.SMEM),
        ],
        out_specs=pl.BlockSpec(memory_space=pltpu.VMEM),
        scratch_shapes=[
            pltpu.VMEM((depth, channels), bf16),
            pltpu.VMEM((points, entries * 128), bf16),
            pltpu.VMEM((entries, out_rows, tile_count * rows), bf16),
            pltpu.VMEM((out_rows, entries * 128), bf16),
            pltpu.VMEM((CHUNKS, tile_count, entries, rows, 128), bf16),
            pltpu.VMEM((CHUNKS, tile_count, entries, rows, 128), bf16),
            pltpu.VMEM((CHUNKS, other, out_rows, part), bf16),
            pltpu.VMEM((CHUNKS, other, out_rows, part), bf16),
            pltpu.VMEM((CHUNKS, other, out_rows, part), bf16),
            pltpu.VMEM((CHUNKS, other, out_rows, part), bf16),
            pltpu.VMEM((CHUNKS, out_rows, part), bf16),
            pltpu.VMEM((CHUNKS, out_rows, part), bf16),
            pltpu.VMEM((CHUNKS, out_rows, part), jnp.float32),
            pltpu.VMEM((out_rows, part), jnp.float32),
            pltpu.VMEM((2 * rows, depth), bf16),
            *[pltpu.VMEM((seg_count * per_seg, rows, 128), bf16) for _ in range(CHUNKS)],
            pltpu.SemaphoreType.DMA((1,)),
            pltpu.SemaphoreType.DMA((entries,)),
            pltpu.SemaphoreType.DMA((2,)),
            pltpu.SemaphoreType.DMA((CHUNKS, 2 * rings)),
            pltpu.SemaphoreType.DMA((CHUNKS, 2 * rings)),
            pltpu.SemaphoreType.DMA((CHUNKS, tile_count)),
            pltpu.SemaphoreType.DMA((CHUNKS, tile_count)),
            pltpu.SemaphoreType.DMA((CHUNKS,)),
            pltpu.SemaphoreType.DMA((CHUNKS, 2 * rings)),
            pltpu.SemaphoreType.DMA((CHUNKS, 2 * rings)),
        ],
        compiler_params=pltpu.CompilerParams(
            collective_id=0, has_side_effects=True, vmem_limit_bytes=60 * 1024 * 1024
        ),
    )(raw, filters, weights, blocks, shifts)
    return image.reshape(1, bank, steps, part)


def solution(mesh):
    return jax.shard_map(
        local,
        mesh=mesh,
        in_specs=(P("tile", "seg"), P(), P("tile", "seg", None, None), P(), P()),
        out_specs=P("tile", None, None, "seg"),
        check_vma=False,
    )
```
